768 devices in a mesh: orb: 8 (over y), grp: 48 (over x, z), aux: 2 (over core).
Axes of the slice: x: 4, y: 8, z: 12, core: 2. Of those that a mesh axis runs over, the one named last changes fastest.
Arguments:
- tiles: bfloat16 [18432, 128, 128], P(('orb', 'grp'), 'aux'), may hold values from -6 to 6
- tile_owner: int32 [18432, 1], P(('orb', 'grp')), may hold values from 0 to 47; in each aligned block of 48 rows (0 to 47, 48 to 95, ...) at most 2 rows name the same one
- tile_panel: int32 [18432], P(('orb', 'grp')), may hold values from 0 to 31
- tile_row: int32 [18432], P(('orb', 'grp')), may hold values from 0 to 11
- density: bfloat16 [32, 48, 128, 128], P('orb', 'grp', 'aux'), may hold values from -0.5 to 0.5
Outputs:
- contracted: float32 [4608, 128, 128], P(('orb', 'grp'), 'aux')
The draws below stay inside these ranges and needn't reach their ends.
Inputs may be any that keep to these rules, and one draw needn't show every extreme that they name: `tile_owner`: in each aligned block of 48 rows (the blocks of one device) no owner appears more than 2 times, and some owner appears exactly 2 times.
All inputs are finite; a program needn't handle non-finite values.
Results may differ from the reference program's by a relative error of at most 0.0029.
Values may be sent and summed in bfloat16 or wider, within the bound.
No kernel may reach another device: no remote copies, remote signals or barrier semaphores. Data moves between devices by JAX's collectives and lax.ppermute only.
A program may use at most 32 MiB of HBM per device.

```python
import math
import jax
import jax.numpy as jnp
import numpy as np
from jax import lax

BLK = 128
JW = 128
KB_DEV = 32
TILES_DEV = 48
ROWS_DEV = 12
CAP = 2
TILES = 18432
N_ORB = 8
N_GRP = 48


def set_ends(values, key, low, high):
    longest = values.shape.index(max(values.shape))
    spots = []
    for shift in (0, 1):
        where = [jax.random.randint(jax.random.fold_in(key, axis), (), 0, length) for axis, length in enumerate(values.shape)]
        where[longest] = (where[longest] + shift) % values.shape[longest]
        spots.append(tuple(where))
    return values.at[spots[0]].set(low).at[spots[1]].set(high)


def levels(own_key, shape, split, low, top_value):
    loudness, own = 1.0, jax.random.fold_in(own_key, 6)
    for axis_at, shards_of in split:
        steps = jnp.exp(jax.random.uniform(jax.random.fold_in(own, axis_at), (shards_of,), jnp.float32, low / len(split), top_value / len(split)))
        loudness = loudness * jnp.repeat(steps, shape[axis_at] // shards_of).reshape([-1 if axis == axis_at else 1 for axis in range(len(shape))])
    return loudness


def routed_block(own_key, own, number, rows, count, top, bound, lean):
    sequence = jax.random.permutation(own_key, count)
    heavy_load, common = portions_of(count, rows * top, bound, lean, True), portions_of(count, rows * top, bound, lean, False)
    places = jnp.arange(count)

    def named(tallies, offset_by):
        used = int((tallies > 0).sum())
        fixed = max(1, used // 4)
        passed = fixed + (places - fixed + offset_by * (used - fixed)) % max(1, count - fixed)
        return jnp.zeros((count,), jnp.int32).at[sequence[jnp.where(places < fixed, places, passed)]].set(jnp.asarray(tallies, jnp.int32))

    tallies = jnp.where(number % 4 == 0, named(heavy_load, number // 4), named(common, number - number // 4 - 1))
    mixed = jax.random.permutation(jax.random.fold_in(own, 3), count)
    donor, sink = mixed[0:count // 2 * 2:2], mixed[1:count // 2 * 2:2]
    room = jnp.minimum(tallies[donor] - 1, bound - tallies[sink]) // 2
    room = jnp.where((donor == sequence[0]) | (sink == sequence[0]) | (tallies[sink] == 0), 0, jnp.maximum(room, 0))
    passed = jax.random.randint(jax.random.fold_in(own, 4), (count // 2,), 0, 1 << 20) % (room + 1)
    tallies = tallies.at[donor].add(-passed).at[sink].add(passed)
    members = jnp.searchsorted(jnp.cumsum(tallies), jnp.arange(rows * top), side="right").astype(jnp.int32)
    grid = members.reshape(top, rows).T
    grid = grid[jax.random.permutation(jax.random.fold_in(own, 1), rows)]
    offset_by = jax.random.randint(jax.random.fold_in(own, 2), (rows, 1), 0, top)
    return jnp.take_along_axis(grid, (jnp.arange(top)[None, :] + offset_by) % top, axis=1)


def portions_of(number_of, total, bound, lean, full):
    weights = [(1 << 20) // math.isqrt(rank ** lean) + 1 for rank in range(1, number_of + 1)]
    largest = bound if full else min(bound, max(-(-total // number_of), total * weights[0] // sum(weights)))
    least = 1 if total - largest >= number_of - 1 else 0
    holding, rest = [largest] + [least] * (number_of - 1), total - largest - least * (number_of - 1)
    while rest > 0:
        candidates = [i for i in range(1, number_of) if holding[i] < largest] or [i for i in range(1, number_of) if holding[i] < bound]
        whole, budget = sum([weights[i] for i in candidates]), rest
        for i in candidates:
            addition = min(bound - holding[i], max(1, budget * weights[i] // whole), rest)
            holding[i] = holding[i] + addition
            rest = rest - addition
    return np.array(holding)


def gaussian(stream_key, shape, deviation, bound, split=(), held_as=jnp.bfloat16):
    loudness = levels(stream_key, shape, split, -0.22, 0.18) if split else 1.0
    values = jax.random.normal(stream_key, shape, jnp.float32) * deviation * loudness
    return jnp.minimum(jnp.maximum(values, -bound), bound).astype(held_as)


def setup_inputs(seed: int = 0) -> dict:
    key_list = jax.random.split(jax.random.key(seed), 6)
    tiles = gaussian(key_list[0], (TILES, BLK, BLK), 1.0, 6.0, ((0, 384), (1, 2)))
    tile_owner_keys = jax.random.split(jax.random.fold_in(key_list[1], 1), TILES // TILES_DEV)
    tile_owner_turns = jax.random.permutation(jax.random.fold_in(key_list[1], 3), TILES // TILES_DEV)
    tile_owner = jax.vmap(lambda own, number: routed_block(jax.random.fold_in(key_list[1], 2), own, number, TILES_DEV, N_GRP, 1, CAP, 2))(tile_owner_keys, tile_owner_turns).reshape((TILES, 1))
    tile_panel = set_ends(jax.random.randint(key_list[2], (TILES,), 0, KB_DEV), jax.random.fold_in(key_list[2], 1), 0, KB_DEV - 1).astype(jnp.int32)
    tile_row = set_ends(jax.random.randint(key_list[3], (TILES,), 0, ROWS_DEV), jax.random.fold_in(key_list[3], 1), 0, ROWS_DEV - 1).astype(jnp.int32)
    density = gaussian(key_list[4], (KB_DEV, N_GRP, BLK, JW), BLK ** -0.5, 0.5, ((0, 8), (1, 48), (2, 2)))
    return {"tiles": tiles, "tile_owner": tile_owner, "tile_panel": tile_panel, "tile_row": tile_row, "density": density}


def reference(tiles, tile_owner, tile_panel, tile_row, density):
    devices_all = N_ORB * N_GRP
    tile_blocks = tiles.reshape(devices_all, TILES_DEV, BLK, BLK)
    owners = tile_owner.reshape(devices_all, TILES_DEV)
    panel_ids = tile_panel.reshape(devices_all, TILES_DEV)
    row_ids = tile_row.reshape(devices_all, TILES_DEV)

    def per_device(items):
        blocks, owner_ids, panel_nums, row_nums = items
        chosen = density[panel_nums, owner_ids]
        products = jnp.einsum("tki,tkj->tij", blocks.astype(jnp.float32), chosen.astype(jnp.float32))
        products = products.astype(jnp.bfloat16).astype(jnp.float32)
        picker = (row_nums[None, :] == jnp.arange(ROWS_DEV, dtype=jnp.int32)[:, None]).astype(jnp.float32)
        summed = jnp.dot(picker, products.reshape(TILES_DEV, BLK * JW), precision=lax.Precision.HIGHEST)
        return summed.reshape(ROWS_DEV, BLK, JW)

    result = lax.map(per_device, (tile_blocks, owners, panel_ids, row_ids))
    return result.reshape(devices_all * ROWS_DEV, BLK, JW)
```

```python
import functools

import jax
import jax.numpy as jnp
from jax import lax
from jax.experimental import pallas as pl
from jax.experimental.pallas import tpu as pltpu
from jax.sharding import Mesh, PartitionSpec as P

Z = 12
PLANE = ("orb", "x")


def pick_kernel(index_ref, table_ref, out_ref):
    def body(i, carry):
        out_ref[i] = table_ref[index_ref[i]]
        return carry

    lax.fori_loop(0, out_ref.shape[0], body, 0, unroll=32)


def sum_kernel(row_ref, core_ref, tiles_ref, panels_ref, out_ref):
    core = core_ref[0]
    half = out_ref.shape[2]
    out_ref[...] = jnp.zeros_like(out_ref)
    for t in range(tiles_ref.shape[0]):
        product = lax.dot_general(
            tiles_ref[t], panels_ref[t], (((0,), (0,)), ((), ())), preferred_element_type=jnp.float32
        )
        row = row_ref[t]
        out_ref[core, row] += product[:half]
        out_ref[1 - core, row] += product[half:]


def shards(tiles, tile_owner, tile_panel, tile_row, density):
    plane = lax.axis_size(PLANE)
    orbs, xs = lax.axis_size("orb"), lax.axis_size("x")
    count, inner, block = tiles.shape
    held = density.shape[0]
    part = inner // plane
    rows_local = count // 4
    owners = tile_owner[:, 0]
    high = (owners % Z) * orbs + tile_panel // held
    low = (owners // Z) * held + tile_panel % held
    asked = jnp.pad(jnp.stack([high, low]).astype(jnp.bfloat16), ((0, 6), (0, 128 - count)))
    slices = density.reshape(held, plane, part, block).transpose(1, 0, 2, 3).reshape(plane, held * part, block)
    outbound = jnp.concatenate([slices, jnp.broadcast_to(asked[None], (plane, 8, 128))], axis=1)
    inbound = lax.all_to_all(outbound, PLANE, 0, 0, tiled=True)
    wanted = inbound[:, held * part : held * part + 2, :count].astype(jnp.int32)
    index = (wanted[:, 0] * (xs * held) + wanted[:, 1]).reshape(-1)
    mine = inbound[:, : held * part]
    table = lax.all_to_all(
        jnp.broadcast_to(mine[None], (Z,) + mine.shape), "z", 0, 0, tiled=True
    )
    picked = pl.pallas_call(
        pick_kernel,
        out_shape=jax.ShapeDtypeStruct((plane * count, part, block), jnp.bfloat16),
        in_specs=[pl.BlockSpec(memory_space=pltpu.SMEM), pl.BlockSpec(memory_space=pltpu.VMEM)],
        out_specs=pl.BlockSpec(memory_space=pltpu.VMEM),
        compiler_params=pltpu.CompilerParams(vmem_limit_bytes=48 * 1024 * 1024),
    )(index, table.reshape(Z * plane * held, part, block))
    panels = lax.all_to_all(picked.reshape(plane, count * part, block), PLANE, 0, 0, tiled=True)
    panels = panels.reshape(plane, count, part, block).transpose(1, 0, 2, 3).reshape(count, inner, block)
    core = lax.axis_index("aux").reshape(1)
    summed = pl.pallas_call(
        sum_kernel,
        out_shape=jax.ShapeDtypeStruct((2, rows_local, block // 2, block), jnp.float32),
        in_specs=[pl.BlockSpec(memory_space=pltpu.SMEM)] * 2 + [pl.BlockSpec(memory_space=pltpu.VMEM)] * 2,
        out_specs=pl.BlockSpec(memory_space=pltpu.VMEM),
        compiler_params=pltpu.CompilerParams(vmem_limit_bytes=48 * 1024 * 1024),
    )(tile_row, core, tiles, panels)
    other = lax.ppermute(summed[1], "aux", [(0, 1), (1, 0)])
    return summed[0] + other


def solution(mesh):
    orbs, grps, cores = mesh.devices.shape
    split = Mesh(mesh.devices.reshape(orbs, grps // Z, Z, cores), ("orb", "x", "z", "aux"))
    own = ("orb", "x", "z")
    return jax.shard_map(
        shards,
        mesh=split,
        in_specs=(
            P(own, "aux", None),
            P(own, None),
            P(own),
            P(own),
            P("orb", ("x", "z"), "aux", None),
        ),
        out_specs=P(own, "aux", None),
        check_vma=False,
    )
```

```python
import functools

import jax
import jax.numpy as jnp
from jax import lax
from jax.experimental import pallas as pl
from jax.experimental.pallas import tpu as pltpu
from jax.sharding import Mesh, PartitionSpec as P

Z = 12
PLANE = ("orb", "x")


def pick_kernel(index_ref, table_ref, out_ref):
    def body(i, carry):
        out_ref[i] = table_ref[index_ref[i]]
        return carry

    lax.fori_loop(0, out_ref.shape[0], body, 0, unroll=32)


def sum_kernel(row_ref, core_ref, tiles_ref, panels_ref, out_ref):
    core = core_ref[0]
    half = out_ref.shape[2]
    out_ref[...] = jnp.zeros_like(out_ref)
    for t in range(tiles_ref.shape[0]):
        product = lax.dot_general(
            tiles_ref[t], panels_ref[t], (((0,), (0,)), ((), ())), preferred_element_type=jnp.float32
        )
        row = row_ref[t]
        out_ref[core, row] += product[:half]
        out_ref[1 - core, row] += product[half:]


def shards(tiles, tile_owner, tile_panel, tile_row, density):
    plane = lax.axis_size(PLANE)
    orbs, xs = lax.axis_size("orb"), lax.axis_size("x")
    count, inner, block = tiles.shape
    held = density.shape[0]
    part = inner // plane
    rows_local = count // 4
    owners = tile_owner[:, 0]
    high = (owners % Z) * orbs + tile_panel // held
    low = (owners // Z) * held + tile_panel % held
    asked = jnp.pad(jnp.stack([high, low]).astype(jnp.bfloat16), ((0, 6), (0, 128 - count)))
    slices = density.reshape(held, plane, part, block).transpose(1, 0, 2, 3).reshape(plane, held * part, block)
    outbound = jnp.concatenate([slices, jnp.broadcast_to(asked[None], (plane, 8, 128))], axis=1)
    inbound = lax.all_to_all(outbound, PLANE, 0, 0, tiled=True)
    wanted = inbound[:, held * part : held * part + 2, :count].astype(jnp.int32)
    index = (wanted[:, 0] * (xs * held) + wanted[:, 1]).reshape(-1)
    mine = inbound[:, : held * part]
    table = lax.all_gather(mine, "z", axis=0, tiled=False)
    picked = pl.pallas_call(
        pick_kernel,
        out_shape=jax.ShapeDtypeStruct((plane * count, part, block), jnp.bfloat16),
        in_specs=[pl.BlockSpec(memory_space=pltpu.SMEM), pl.BlockSpec(memory_space=pltpu.VMEM)],
        out_specs=pl.BlockSpec(memory_space=pltpu.VMEM),
        compiler_params=pltpu.CompilerParams(vmem_limit_bytes=48 * 1024 * 1024),
    )(index, table.reshape(Z * plane * held, part, block))
    panels = lax.all_to_all(picked.reshape(plane, count * part, block), PLANE, 0, 0, tiled=True)
    panels = panels.reshape(plane, count, part, block).transpose(1, 0, 2, 3).reshape(count, inner, block)
    core = lax.axis_index("aux").reshape(1)
    summed = pl.pallas_call(
        sum_kernel,
        out_shape=jax.ShapeDtypeStruct((2, rows_local, block // 2, block), jnp.float32),
        in_specs=[pl.BlockSpec(memory_space=pltpu.SMEM)] * 2 + [pl.BlockSpec(memory_space=pltpu.VMEM)] * 2,
        out_specs=pl.BlockSpec(memory_space=pltpu.VMEM),
        compiler_params=pltpu.CompilerParams(vmem_limit_bytes=48 * 1024 * 1024),
    )(tile_row, core, tiles, panels)
    other = lax.ppermute(summed[1], "aux", [(0, 1), (1, 0)])
    return summed[0] + other


def solution(mesh):
    orbs, grps, cores = mesh.devices.shape
    split = Mesh(mesh.devices.reshape(orbs, grps // Z, Z, cores), ("orb", "x", "z", "aux"))
    own = ("orb", "x", "z")
    return jax.shard_map(
        shards,
        mesh=split,
        in_specs=(
            P(own, "aux", None),
            P(own, None),
            P(own),
            P(own),
            P("orb", ("x", "z"), "aux", None),
        ),
        out_specs=P(own, "aux", None),
        check_vma=False,
    )
```

```python
import jax
import jax.numpy as jnp
from jax import lax
from jax.experimental import pallas as pl
from jax.experimental.pallas import tpu as pltpu
from jax.sharding import Mesh, PartitionSpec as P

Z = 12
PLANE = ("orb", "x")


def pick_kernel(index_hbm, table_ref, out_hbm, index_ref, out_ref, in_sem, out_sem):
    pieces = in_sem.shape[0]
    lines, width = index_ref.shape
    per = lines // pieces
    fetches, sends = [], []
    for piece in range(pieces):
        span = pl.ds(piece * per, per)
        fetches.append(pltpu.make_async_copy(index_hbm.at[span], index_ref.at[span], in_sem.at[piece]))
        fetches[-1].start()
    for piece in range(pieces):
        fetches[piece].wait()

        def body(line, carry):
            for i in range(width):
                out_ref[line * width + i] = table_ref[index_ref[line, i]]
            return carry

        lax.fori_loop(piece * per, (piece + 1) * per, body, 0)
        span = pl.ds(piece * per * width, per * width)
        sends.append(pltpu.make_async_copy(out_ref.at[span], out_hbm.at[span], out_sem.at[piece]))
        sends[-1].start()
    for send in sends:
        send.wait()


def turn_kernel(core_ref, row_ref, tiles_ref, sent_ref, kept_ref, near_row_ref):
    half = sent_ref.shape[1]
    first = core_ref[0] == 0
    near_row_ref[...] = row_ref[...]

    def body(t, carry):
        turned = tiles_ref[t].T
        sent_ref[t] = jnp.where(first, turned[half:], turned[:half])
        kept_ref[t] = jnp.where(first, turned[:half], turned[half:])
        return carry

    lax.fori_loop(0, tiles_ref.shape[0], body, 0, unroll=4)


def sum_kernel(row_vmem, turned_ref, panels_ref, out_ref, row_ref, product_ref, row_sem):
    fetch = pltpu.make_async_copy(row_vmem, row_ref, row_sem)
    fetch.start()
    count, _, inner = turned_ref.shape
    out_ref[...] = jnp.zeros_like(out_ref)
    for t in range(count):
        panel = panels_ref[:, t].reshape(inner, out_ref.shape[2])
        product_ref[t] = jnp.dot(turned_ref[t], panel, preferred_element_type=jnp.float32)
    fetch.wait()
    for t in range(count):
        out_ref[row_ref[0, t]] += product_ref[t]


def shards(tiles, tile_owner, tile_panel, tile_row, density):
    plane = lax.axis_size(PLANE)
    xs = lax.axis_size("x")
    count, inner, block = tiles.shape
    held = density.shape[0]
    part = inner // plane
    rows_local = count // 4
    owners = tile_owner[:, 0]
    high = (owners % Z) * lax.axis_size("orb") + tile_panel // held
    low = (owners // Z) * held + tile_panel % held
    asked = jnp.pad(jnp.stack([high, low]).astype(jnp.bfloat16), ((0, 6), (0, block - count)))
    slices = density.reshape(held, plane, part, block).transpose(1, 0, 2, 3).reshape(plane, held * part, block)
    outbound = jnp.concatenate([slices, jnp.broadcast_to(asked[None], (plane, 8, block))], axis=1)
    inbound = lax.all_to_all(outbound, PLANE, 0, 0, tiled=True)
    wanted = inbound[:, held * part : held * part + 2, :count].astype(jnp.int32)
    index = (wanted[:, 0] * (xs * held) + wanted[:, 1]).reshape(-1)
    mine = inbound[:, : held * part]
    table = lax.all_gather(mine, "z", axis=0, tiled=False)
    pieces = 12
    picked = pl.pallas_call(
        pick_kernel,
        out_shape=jax.ShapeDtypeStruct((plane * count, part, block), jnp.bfloat16),
        in_specs=[pl.BlockSpec(memory_space=pl.ANY), pl.BlockSpec(memory_space=pltpu.VMEM)],
        out_specs=pl.BlockSpec(memory_space=pl.ANY),
        scratch_shapes=[
            pltpu.SMEM((plane * count // 128, 128), jnp.int32),
            pltpu.VMEM((plane * count, part, block), jnp.bfloat16),
            pltpu.SemaphoreType.DMA((pieces,)),
            pltpu.SemaphoreType.DMA((pieces,)),
        ],
        compiler_params=pltpu.CompilerParams(vmem_limit_bytes=16 * 1024 * 1024),
    )(index.reshape(-1, 128), table.reshape(Z * plane * held, part, block))
    panels = lax.all_to_all(picked.reshape(plane, count * part, block), PLANE, 0, 0, tiled=True)
    panels = panels.reshape(plane, count, part, block)
    half = block // 2
    core = lax.axis_index("aux").reshape(1)
    sent, kept, near_row = pl.pallas_call(
        turn_kernel,
        out_shape=[jax.ShapeDtypeStruct((count, half, inner), jnp.bfloat16)] * 2
        + [jax.ShapeDtypeStruct((1, count), jnp.int32)],
        in_specs=[pl.BlockSpec(memory_space=pltpu.SMEM)] + [pl.BlockSpec(memory_space=pltpu.VMEM)] * 2,
        out_specs=[pl.BlockSpec(memory_space=pltpu.VMEM)] * 3,
        cost_estimate=pl.CostEstimate(flops=0, bytes_accessed=4 * tiles.size, transcendentals=0),
        compiler_params=pltpu.CompilerParams(vmem_limit_bytes=8 * 1024 * 1024),
    )(core, tile_row.reshape(1, count), tiles)

    def row_sums(turned):
        return pl.pallas_call(
            sum_kernel,
            out_shape=jax.ShapeDtypeStruct((rows_local, half, block), jnp.float32),
            in_specs=[pl.BlockSpec(memory_space=pltpu.VMEM)] * 3,
            out_specs=pl.BlockSpec(memory_space=pltpu.VMEM),
            scratch_shapes=[
                pltpu.SMEM((1, count), jnp.int32),
                pltpu.VMEM((count, half, block), jnp.float32),
                pltpu.SemaphoreType.DMA,
            ],
            cost_estimate=pl.CostEstimate(
                flops=2 * tiles.size * half, bytes_accessed=4 * tiles.size, transcendentals=0
            ),
            compiler_params=pltpu.CompilerParams(vmem_limit_bytes=16 * 1024 * 1024),
        )(near_row, turned, panels)

    other = lax.ppermute(row_sums(sent), "aux", [(0, 1), (1, 0)])
    return row_sums(kept) + other


def solution(mesh):
    orbs, grps, cores = mesh.devices.shape
    split = Mesh(mesh.devices.reshape(orbs, grps // Z, Z, cores), ("orb", "x", "z", "aux"))
    own = ("orb", "x", "z")
    return jax.shard_map(
        shards,
        mesh=split,
        in_specs=(
            P(own, "aux", None),
            P(own, None),
            P(own),
            P(own),
            P("orb", ("x", "z"), "aux", None),
        ),
        out_specs=P(own, "aux", None),
        check_vma=False,
    )
```

```python
import jax
import jax.numpy as jnp
from jax import lax
from jax.experimental import pallas as pl
from jax.experimental.pallas import tpu as pltpu
from jax.sharding import Mesh, PartitionSpec as P

Z = 12
PLANE = ("orb", "x")
TURN = (4, 2)


def numbered(orbs, xs):
    return [[(i // xs + TURN[0]) % orbs * xs + (i + TURN[1]) % xs for i in range(orbs * xs)]]


def pick_kernel(index_hbm, table_ref, out_hbm, index_ref, out_ref, in_sem, out_sem):
    pieces = in_sem.shape[0]
    lines, width = index_ref.shape
    per = lines // pieces
    fetches, sends = [], []
    for piece in range(pieces):
        span = pl.ds(piece * per, per)
        fetches.append(pltpu.make_async_copy(index_hbm.at[span], index_ref.at[span], in_sem.at[piece]))
        fetches[-1].start()
    for piece in range(pieces):
        fetches[piece].wait()

        def body(line, carry):
            for i in range(width):
                out_ref[line * width + i] = table_ref[index_ref[line, i]]
            return carry

        lax.fori_loop(piece * per, (piece + 1) * per, body, 0)
        span = pl.ds(piece * per * width, per * width)
        sends.append(pltpu.make_async_copy(out_ref.at[span], out_hbm.at[span], out_sem.at[piece]))
        sends[-1].start()
    for send in sends:
        send.wait()


def turn_kernel(core_ref, row_ref, tiles_ref, sent_ref, kept_ref, near_row_ref):
    half = sent_ref.shape[1]
    first = core_ref[0] == 0
    near_row_ref[...] = row_ref[...]

    def body(t, carry):
        turned = tiles_ref[t].T
        sent_ref[t] = jnp.where(first, turned[half:], turned[:half])
        kept_ref[t] = jnp.where(first, turned[:half], turned[half:])
        return carry

    lax.fori_loop(0, tiles_ref.shape[0], body, 0, unroll=4)


def sum_kernel(row_vmem, turned_ref, panels_ref, out_ref, row_ref, product_ref, row_sem):
    fetch = pltpu.make_async_copy(row_vmem, row_ref, row_sem)
    fetch.start()
    count, _, inner = turned_ref.shape
    out_ref[...] = jnp.zeros_like(out_ref)
    for t in range(count):
        panel = panels_ref[:, t].reshape(inner, out_ref.shape[2])
        product_ref[t] = jnp.dot(turned_ref[t], panel, preferred_element_type=jnp.float32)
    fetch.wait()
    for t in range(count):
        out_ref[row_ref[0, t]] += product_ref[t]


def shards(tiles, tile_owner, tile_panel, tile_row, density):
    plane = lax.axis_size(PLANE)
    orbs, xs = lax.axis_size("orb"), lax.axis_size("x")
    order = numbered(orbs, xs)
    count, inner, block = tiles.shape
    held = density.shape[0]
    part = inner // plane
    rows_local = count // 4
    owners = tile_owner[:, 0]
    high = (Z - 1 - owners % Z) * orbs + (tile_panel // held - TURN[0]) % orbs
    low = (owners // Z - TURN[1]) % xs * held + tile_panel % held
    asked = jnp.pad(jnp.stack([high, low]).astype(jnp.bfloat16), ((0, 6), (0, block - count)))
    slices = density.reshape(held, plane, part, block).transpose(1, 0, 2, 3).reshape(plane, held * part, block)
    outbound = jnp.concatenate([slices, jnp.broadcast_to(asked[None], (plane, 8, block))], axis=1)
    inbound = lax.all_to_all(outbound, PLANE, 0, 0, axis_index_groups=order, tiled=True)
    wanted = inbound[:, held * part : held * part + 2, :count].astype(jnp.int32)
    index = (wanted[:, 0] * (xs * held) + wanted[:, 1]).reshape(-1)
    mine = inbound[:, : held * part]
    table = lax.all_gather(mine, "z", axis=0, axis_index_groups=[list(range(Z))[::-1]], tiled=False)
    pieces = 12
    picked = pl.pallas_call(
        pick_kernel,
        out_shape=jax.ShapeDtypeStruct((plane * count, part, block), jnp.bfloat16),
        in_specs=[pl.BlockSpec(memory_space=pl.ANY), pl.BlockSpec(memory_space=pltpu.VMEM)],
        out_specs=pl.BlockSpec(memory_space=pl.ANY),
        scratch_shapes=[
            pltpu.SMEM((plane * count // 128, 128), jnp.int32),
            pltpu.VMEM((plane * count, part, block), jnp.bfloat16),
            pltpu.SemaphoreType.DMA((pieces,)),
            pltpu.SemaphoreType.DMA((pieces,)),
        ],
        compiler_params=pltpu.CompilerParams(vmem_limit_bytes=16 * 1024 * 1024),
    )(index.reshape(-1, 128), table.reshape(Z * plane * held, part, block))
    panels = lax.all_to_all(picked.reshape(plane, count * part, block), PLANE, 0, 0, axis_index_groups=order, tiled=True)
    panels = panels.reshape(plane, count, part, block)
    half = block // 2
    core = lax.axis_index("aux").reshape(1)
    sent, kept, near_row = pl.pallas_call(
        turn_kernel,
        out_shape=[jax.ShapeDtypeStruct((count, half, inner), jnp.bfloat16)] * 2
        + [jax.ShapeDtypeStruct((1, count), jnp.int32)],
        in_specs=[pl.BlockSpec(memory_space=pltpu.SMEM)] + [pl.BlockSpec(memory_space=pltpu.VMEM)] * 2,
        out_specs=[pl.BlockSpec(memory_space=pltpu.VMEM)] * 3,
        cost_estimate=pl.CostEstimate(flops=0, bytes_accessed=4 * tiles.size, transcendentals=0),
        compiler_params=pltpu.CompilerParams(vmem_limit_bytes=8 * 1024 * 1024),
    )(core, tile_row.reshape(1, count), tiles)

    def row_sums(turned):
        return pl.pallas_call(
            sum_kernel,
            out_shape=jax.ShapeDtypeStruct((rows_local, half, block), jnp.float32),
            in_specs=[pl.BlockSpec(memory_space=pltpu.VMEM)] * 3,
            out_specs=pl.BlockSpec(memory_space=pltpu.VMEM),
            scratch_shapes=[
                pltpu.SMEM((1, count), jnp.int32),
                pltpu.VMEM((count, half, block), jnp.float32),
                pltpu.SemaphoreType.DMA,
            ],
            cost_estimate=pl.CostEstimate(
                flops=2 * tiles.size * half, bytes_accessed=4 * tiles.size, transcendentals=0
            ),
            compiler_params=pltpu.CompilerParams(vmem_limit_bytes=16 * 1024 * 1024),
        )(near_row, turned, panels)

    other = lax.ppermute(row_sums(sent), "aux", [(0, 1), (1, 0)])
    return row_sums(kept) + other


def solution(mesh):
    orbs, grps, cores = mesh.devices.shape
    split = Mesh(mesh.devices.reshape(orbs, grps // Z, Z, cores), ("orb", "x", "z", "aux"))
    own = ("orb", "x", "z")
    return jax.shard_map(
        shards,
        mesh=split,
        in_specs=(
            P(own, "aux", None),
            P(own, None),
            P(own),
            P(own),
            P("orb", ("x", "z"), "aux", None),
        ),
        out_specs=P(own, "aux", None),
        check_vma=False,
    )
```

```python
import jax
import jax.numpy as jnp
from jax import lax
from jax.experimental import pallas as pl
from jax.experimental.pallas import tpu as pltpu
from jax.sharding import Mesh, PartitionSpec as P

Z = 12
PLANE = ("orb", "x")
TURN = (4, 2)


def numbered(orbs, xs):
    return [[(i // xs + TURN[0]) % orbs * xs + (i + TURN[1]) % xs for i in range(orbs * xs)]]


IN_PARTS = (1, 3, 8)
OUT_PARTS = (5, 4, 2, 1)


def spans(lines, parts):
    edges = [lines * sum(parts[:i]) // sum(parts) for i in range(len(parts) + 1)]
    return list(zip(edges[:-1], edges[1:]))


def pick_kernel(index_hbm, table_ref, out_hbm, index_ref, out_ref, in_sem, out_sem):
    lines, width = index_ref.shape
    fetches, sends = {}, []
    for piece, (start, stop) in enumerate(spans(lines, IN_PARTS)):
        span = pl.ds(start, stop - start)
        fetches[start] = pltpu.make_async_copy(index_hbm.at[span], index_ref.at[span], in_sem.at[piece])
        fetches[start].start()
    outs = spans(lines, OUT_PARTS)
    for line in range(lines):
        if line in fetches:
            fetches[line].wait()
        for i in range(width):
            out_ref[line * width + i] = table_ref[index_ref[line, i]]
        if line + 1 == outs[len(sends)][1]:
            start = outs[len(sends)][0] * width
            span = pl.ds(start, (line + 1) * width - start)
            sends.append(pltpu.make_async_copy(out_ref.at[span], out_hbm.at[span], out_sem.at[len(sends)]))
            sends[-1].start()
    for send in sends:
        send.wait()


def turn_kernel(core_ref, row_ref, tiles_ref, sent_ref, kept_ref, near_row_ref):
    half = sent_ref.shape[1]
    first = core_ref[0] == 0
    near_row_ref[...] = row_ref[...]

    def body(t, carry):
        turned = tiles_ref[t].T
        sent_ref[t] = jnp.where(first, turned[half:], turned[:half])
        kept_ref[t] = jnp.where(first, turned[:half], turned[half:])
        return carry

    lax.fori_loop(0, tiles_ref.shape[0], body, 0, unroll=4)


def sum_kernel(row_vmem, turned_ref, panels_ref, out_ref, row_ref, product_ref, row_sem):
    fetch = pltpu.make_async_copy(row_vmem, row_ref, row_sem)
    fetch.start()
    count, _, inner = turned_ref.shape
    out_ref[...] = jnp.zeros_like(out_ref)
    for t in range(count):
        panel = panels_ref[:, t].reshape(inner, out_ref.shape[2])
        product_ref[t] = jnp.dot(turned_ref[t], panel, preferred_element_type=jnp.float32)
    fetch.wait()
    for t in range(count):
        out_ref[row_ref[0, t]] += product_ref[t]


def shards(tiles, tile_owner, tile_panel, tile_row, density):
    plane = lax.axis_size(PLANE)
    orbs, xs = lax.axis_size("orb"), lax.axis_size("x")
    order = numbered(orbs, xs)
    count, inner, block = tiles.shape
    held = density.shape[0]
    part = inner // plane
    rows_local = count // 4
    owners = tile_owner[:, 0]
    high = (Z - 1 - owners % Z) * orbs + (tile_panel // held - TURN[0]) % orbs
    low = (owners // Z - TURN[1]) % xs * held + tile_panel % held
    asked = jnp.pad(jnp.stack([high, low]).astype(jnp.bfloat16), ((0, 6), (0, block - count)))
    slices = density.reshape(held, plane, part, block).transpose(1, 0, 2, 3).reshape(plane, held * part, block)
    outbound = jnp.concatenate([slices, jnp.broadcast_to(asked[None], (plane, 8, block))], axis=1)
    inbound = lax.all_to_all(outbound, PLANE, 0, 0, axis_index_groups=order, tiled=True)
    wanted = inbound[:, held * part : held * part + 2, :count].astype(jnp.int32)
    index = (wanted[:, 0] * (xs * held) + wanted[:, 1]).reshape(-1)
    mine = inbound[:, : held * part]
    table = lax.all_gather(mine, "z", axis=0, axis_index_groups=[list(range(Z))[::-1]], tiled=False)
    picked = pl.pallas_call(
        pick_kernel,
        out_shape=jax.ShapeDtypeStruct((plane * count, part, block), jnp.bfloat16),
        in_specs=[pl.BlockSpec(memory_space=pl.ANY), pl.BlockSpec(memory_space=pltpu.VMEM)],
        out_specs=pl.BlockSpec(memory_space=pl.ANY),
        scratch_shapes=[
            pltpu.SMEM((plane * count // 128, 128), jnp.int32),
            pltpu.VMEM((plane * count, part, block), jnp.bfloat16),
            pltpu.SemaphoreType.DMA((len(IN_PARTS),)),
            pltpu.SemaphoreType.DMA((len(OUT_PARTS),)),
        ],
        compiler_params=pltpu.CompilerParams(vmem_limit_bytes=16 * 1024 * 1024),
    )(index.reshape(-1, 128), table.reshape(Z * plane * held, part, block))
    panels = lax.all_to_all(picked.reshape(plane, count * part, block), PLANE, 0, 0, axis_index_groups=order, tiled=True)
    panels = panels.reshape(plane, count, part, block)
    half = block // 2
    core = lax.axis_index("aux").reshape(1)
    sent, kept, near_row = pl.pallas_call(
        turn_kernel,
        out_shape=[jax.ShapeDtypeStruct((count, half, inner), jnp.bfloat16)] * 2
        + [jax.ShapeDtypeStruct((1, count), jnp.int32)],
        in_specs=[pl.BlockSpec(memory_space=pltpu.SMEM)] + [pl.BlockSpec(memory_space=pltpu.VMEM)] * 2,
        out_specs=[pl.BlockSpec(memory_space=pltpu.VMEM)] * 3,
        cost_estimate=pl.CostEstimate(flops=0, bytes_accessed=4 * tiles.size, transcendentals=0),
        compiler_params=pltpu.CompilerParams(vmem_limit_bytes=8 * 1024 * 1024),
    )(core, tile_row.reshape(1, count), tiles)

    def row_sums(turned):
        return pl.pallas_call(
            sum_kernel,
            out_shape=jax.ShapeDtypeStruct((rows_local, half, block), jnp.float32),
            in_specs=[pl.BlockSpec(memory_space=pltpu.VMEM)] * 3,
            out_specs=pl.BlockSpec(memory_space=pltpu.VMEM),
            scratch_shapes=[
                pltpu.SMEM((1, count), jnp.int32),
                pltpu.VMEM((count, half, block), jnp.float32),
                pltpu.SemaphoreType.DMA,
            ],
            cost_estimate=pl.CostEstimate(
                flops=2 * tiles.size * half, bytes_accessed=4 * tiles.size, transcendentals=0
            ),
            compiler_params=pltpu.CompilerParams(vmem_limit_bytes=16 * 1024 * 1024),
        )(near_row, turned, panels)

    other = lax.ppermute(row_sums(sent), "aux", [(0, 1), (1, 0)])
    return row_sums(kept) + other


def solution(mesh):
    orbs, grps, cores = mesh.devices.shape
    split = Mesh(mesh.devices.reshape(orbs, grps // Z, Z, cores), ("orb", "x", "z", "aux"))
    own = ("orb", "x", "z")
    return jax.shard_map(
        shards,
        mesh=split,
        in_specs=(
            P(own, "aux", None),
            P(own, None),
            P(own),
            P(own),
            P("orb", ("x", "z"), "aux", None),
        ),
        out_specs=P(own, "aux", None),
        check_vma=False,
    )
```

```python
import jax
import jax.numpy as jnp
from jax import lax
from jax.experimental import pallas as pl
from jax.experimental.pallas import tpu as pltpu
from jax.sharding import Mesh, PartitionSpec as P

Z = 12
PLANE = ("orb", "x")
TURN = (5, 2)


def numbered(orbs, xs):
    return [[(i // xs + TURN[0]) % orbs * xs + (i + TURN[1]) % xs for i in range(orbs * xs)]]


IN_PARTS = (1, 3, 8)
OUT_PARTS = (5, 4, 2, 1)


def spans(lines, parts):
    edges = [lines * sum(parts[:i]) // sum(parts) for i in range(len(parts) + 1)]
    return list(zip(edges[:-1], edges[1:]))


ORDER2 = [[(4 + i // 4) % 8 * 4 + (2 + i) % 4 for i in range(32)]]


def pick_kernel(index_hbm, table_ref, out_hbm, index_ref, out_ref, in_sem, out_sem):
    lines, width = index_ref.shape
    fetches, sends = {}, []
    for piece, (start, stop) in enumerate(spans(lines, IN_PARTS)):
        span = pl.ds(start, stop - start)
        fetches[start] = pltpu.make_async_copy(index_hbm.at[span], index_ref.at[span], in_sem.at[piece])
        fetches[start].start()
    outs = spans(lines, OUT_PARTS)
    for line in range(lines):
        if line in fetches:
            fetches[line].wait()
        for i in range(width):
            out_ref[line * width + i] = table_ref[index_ref[line, i]]
        if line + 1 == outs[len(sends)][1]:
            start = outs[len(sends)][0] * width
            span = pl.ds(start, (line + 1) * width - start)
            sends.append(pltpu.make_async_copy(out_ref.at[span], out_hbm.at[span], out_sem.at[len(sends)]))
            sends[-1].start()
    for send in sends:
        send.wait()


def turn_kernel(core_ref, row_ref, tiles_ref, sent_ref, kept_ref, near_row_ref):
    half = sent_ref.shape[1]
    first = core_ref[0] == 0
    near_row_ref[...] = row_ref[...]

    def body(t, carry):
        turned = tiles_ref[t].T
        sent_ref[t] = jnp.where(first, turned[half:], turned[:half])
        kept_ref[t] = jnp.where(first, turned[:half], turned[half:])
        return carry

    lax.fori_loop(0, tiles_ref.shape[0], body, 0, unroll=4)


def sum_kernel(row_vmem, turned_ref, panels_ref, out_ref, row_ref, product_ref, row_sem):
    fetch = pltpu.make_async_copy(row_vmem, row_ref, row_sem)
    fetch.start()
    count, _, inner = turned_ref.shape
    out_ref[...] = jnp.zeros_like(out_ref)
    for t in range(count):
        panel = panels_ref[:, t].reshape(inner, out_ref.shape[2])
        product_ref[t] = jnp.dot(turned_ref[t], panel, preferred_element_type=jnp.float32)
    fetch.wait()
    for t in range(count):
        out_ref[row_ref[0, t]] += product_ref[t]


def shards(tiles, tile_owner, tile_panel, tile_row, density):
    plane = lax.axis_size(PLANE)
    orbs, xs = lax.axis_size("orb"), lax.axis_size("x")
    order = numbered(orbs, xs)
    count, inner, block = tiles.shape
    held = density.shape[0]
    part = inner // plane
    rows_local = count // 4
    owners = tile_owner[:, 0]
    high = (Z - 1 - owners % Z) * orbs + (tile_panel // held - TURN[0]) % orbs
    low = (owners // Z - TURN[1]) % xs * held + tile_panel % held
    asked = jnp.pad(jnp.stack([high, low]).astype(jnp.bfloat16), ((0, 6), (0, block - count)))
    slices = density.reshape(held, plane, part, block).transpose(1, 0, 2, 3).reshape(plane, held * part, block)
    outbound = jnp.concatenate([slices, jnp.broadcast_to(asked[None], (plane, 8, block))], axis=1)
    inbound = lax.all_to_all(outbound, PLANE, 0, 0, axis_index_groups=order, tiled=True)
    wanted = inbound[:, held * part : held * part + 2, :count].astype(jnp.int32)
    wanted = jnp.roll(wanted.reshape(8, 4, 2, count), 1, 0).reshape(32, 2, count)
    tiles = jnp.roll(tiles.reshape(count, 8, 8, block), 1, 1).reshape(count, inner, block)
    index = (wanted[:, 0] * (xs * held) + wanted[:, 1]).reshape(-1)
    mine = inbound[:, : held * part]
    table = lax.all_gather(mine, "z", axis=0, axis_index_groups=[list(range(Z))[::-1]], tiled=False)
    picked = pl.pallas_call(
        pick_kernel,
        out_shape=jax.ShapeDtypeStruct((plane * count, part, block), jnp.bfloat16),
        in_specs=[pl.BlockSpec(memory_space=pl.ANY), pl.BlockSpec(memory_space=pltpu.VMEM)],
        out_specs=pl.BlockSpec(memory_space=pl.ANY),
        scratch_shapes=[
            pltpu.SMEM((plane * count // 128, 128), jnp.int32),
            pltpu.VMEM((plane * count, part, block), jnp.bfloat16),
            pltpu.SemaphoreType.DMA((len(IN_PARTS),)),
            pltpu.SemaphoreType.DMA((len(OUT_PARTS),)),
        ],
        compiler_params=pltpu.CompilerParams(vmem_limit_bytes=16 * 1024 * 1024),
    )(index.reshape(-1, 128), table.reshape(Z * plane * held, part, block))
    panels = lax.all_to_all(picked.reshape(plane, count * part, block), PLANE, 0, 0, axis_index_groups=ORDER2, tiled=True)
    panels = panels.reshape(plane, count, part, block)
    half = block // 2
    core = lax.axis_index("aux").reshape(1)
    sent, kept, near_row = pl.pallas_call(
        turn_kernel,
        out_shape=[jax.ShapeDtypeStruct((count, half, inner), jnp.bfloat16)] * 2
        + [jax.ShapeDtypeStruct((1, count), jnp.int32)],
        in_specs=[pl.BlockSpec(memory_space=pltpu.SMEM)] + [pl.BlockSpec(memory_space=pltpu.VMEM)] * 2,
        out_specs=[pl.BlockSpec(memory_space=pltpu.VMEM)] * 3,
        cost_estimate=pl.CostEstimate(flops=0, bytes_accessed=4 * tiles.size, transcendentals=0),
        compiler_params=pltpu.CompilerParams(vmem_limit_bytes=8 * 1024 * 1024),
    )(core, tile_row.reshape(1, count), tiles)

    def row_sums(turned):
        return pl.pallas_call(
            sum_kernel,
            out_shape=jax.ShapeDtypeStruct((rows_local, half, block), jnp.float32),
            in_specs=[pl.BlockSpec(memory_space=pltpu.VMEM)] * 3,
            out_specs=pl.BlockSpec(memory_space=pltpu.VMEM),
            scratch_shapes=[
                pltpu.SMEM((1, count), jnp.int32),
                pltpu.VMEM((count, half, block), jnp.float32),
                pltpu.SemaphoreType.DMA,
            ],
            cost_estimate=pl.CostEstimate(
                flops=2 * tiles.size * half, bytes_accessed=4 * tiles.size, transcendentals=0
            ),
            compiler_params=pltpu.CompilerParams(vmem_limit_bytes=16 * 1024 * 1024),
        )(near_row, turned, panels)

    other = lax.ppermute(row_sums(sent), "aux", [(0, 1), (1, 0)])
    return row_sums(kept) + other


def solution(mesh):
    orbs, grps, cores = mesh.devices.shape
    split = Mesh(mesh.devices.reshape(orbs, grps // Z, Z, cores), ("orb", "x", "z", "aux"))
    own = ("orb", "x", "z")
    return jax.shard_map(
        shards,
        mesh=split,
        in_specs=(
            P(own, "aux", None),
            P(own, None),
            P(own),
            P(own),
            P("orb", ("x", "z"), "aux", None),
        ),
        out_specs=P(own, "aux", None),
        check_vma=False,
    )
```

```python
import jax
import jax.numpy as jnp
from jax import lax
from jax.experimental import pallas as pl
from jax.experimental.pallas import tpu as pltpu
from jax.sharding import Mesh, PartitionSpec as P

Z = 12
PLANE = ("orb", "x")
TURN = (5, 2)


def numbered(orbs, xs):
    return [[(i // xs + TURN[0]) % orbs * xs + (i + TURN[1]) % xs for i in range(orbs * xs)]]


IN_PARTS = (1, 3, 8)
OUT_PARTS = (5, 4, 2, 1)


def spans(lines, parts):
    edges = [lines * sum(parts[:i]) // sum(parts) for i in range(len(parts) + 1)]
    return list(zip(edges[:-1], edges[1:]))


ORDER2 = [[(4 + i // 4) % 8 * 4 + (2 + i) % 4 for i in range(32)]]


def pick_kernel(index_hbm, table_ref, out_hbm, index_ref, out_ref, in_sem, out_sem):
    lines, width = index_ref.shape
    fetches, sends = {}, []
    for piece, (start, stop) in enumerate(spans(lines, IN_PARTS)):
        span = pl.ds(start, stop - start)
        fetches[start] = pltpu.make_async_copy(index_hbm.at[span], index_ref.at[span], in_sem.at[piece])
        fetches[start].start()
    outs = spans(lines, OUT_PARTS)
    for line in range(lines):
        if line in fetches:
            fetches[line].wait()
        for i in range(width):
            out_ref[line * width + i] = table_ref[index_ref[line, i]]
        if line + 1 == outs[len(sends)][1]:
            start = outs[len(sends)][0] * width
            span = pl.ds(start, (line + 1) * width - start)
            sends.append(pltpu.make_async_copy(out_ref.at[span], out_hbm.at[span], out_sem.at[len(sends)]))
            sends[-1].start()
    for send in sends:
        send.wait()


def turn_kernel(core_ref, row_ref, tiles_ref, sent_ref, kept_ref, near_row_ref):
    half = sent_ref.shape[1]
    first = core_ref[0] == 0
    near_row_ref[...] = row_ref[...]

    def body(t, carry):
        turned = tiles_ref[t].T
        sent_ref[t] = jnp.where(first, turned[half:], turned[:half])
        kept_ref[t] = jnp.where(first, turned[:half], turned[half:])
        return carry

    lax.fori_loop(0, tiles_ref.shape[0], body, 0, unroll=4)


def sum_kernel(row_vmem, turned_ref, panels_ref, out_ref, row_ref, product_ref, row_sem):
    fetch = pltpu.make_async_copy(row_vmem, row_ref, row_sem)
    fetch.start()
    count, _, inner = turned_ref.shape
    out_ref[...] = jnp.zeros_like(out_ref)
    for t in range(count):
        panel = panels_ref[:, t].reshape(inner, out_ref.shape[2])
        product_ref[t] = jnp.dot(turned_ref[t], panel, preferred_element_type=jnp.float32)
    fetch.wait()
    for t in range(count):
        out_ref[row_ref[0, t]] += product_ref[t]


def shards(tiles, tile_owner, tile_panel, tile_row, density):
    plane = lax.axis_size(PLANE)
    orbs, xs = lax.axis_size("orb"), lax.axis_size("x")
    order = numbered(orbs, xs)
    count, inner, block = tiles.shape
    held = density.shape[0]
    part = inner // plane
    rows_local = count // 4
    owners = tile_owner[:, 0]
    high = (Z - 1 - owners % Z) * orbs + (tile_panel // held - TURN[0]) % orbs
    low = (owners // Z - TURN[1]) % xs * held + tile_panel % held
    asked = jnp.pad(jnp.stack([high, low]).astype(jnp.bfloat16), ((0, 0), (0, block - count)))
    slices = density.reshape(held, plane, part, block).transpose(1, 0, 2, 3).reshape(plane, held * part, block)
    outbound = jnp.concatenate([slices, jnp.broadcast_to(asked[None], (plane, 2, block))], axis=1)
    inbound = lax.all_to_all(outbound, PLANE, 0, 0, axis_index_groups=order, tiled=True)
    wanted = inbound[:, held * part : held * part + 2, :count].astype(jnp.int32)
    wanted = jnp.roll(wanted.reshape(8, 4, 2, count), 1, 0).reshape(32, 2, count)
    tiles = jnp.roll(tiles.reshape(count, 8, 8, block), 1, 1).reshape(count, inner, block)
    index = (wanted[:, 0] * (xs * held) + wanted[:, 1]).reshape(-1)
    mine = inbound[:, : held * part]
    table = lax.all_gather(mine, "z", axis=0, axis_index_groups=[list(range(Z))[::-1]], tiled=False)
    picked = pl.pallas_call(
        pick_kernel,
        out_shape=jax.ShapeDtypeStruct((plane * count, part, block), jnp.bfloat16),
        in_specs=[pl.BlockSpec(memory_space=pl.ANY), pl.BlockSpec(memory_space=pltpu.VMEM)],
        out_specs=pl.BlockSpec(memory_space=pl.ANY),
        scratch_shapes=[
            pltpu.SMEM((plane * count // 128, 128), jnp.int32),
            pltpu.VMEM((plane * count, part, block), jnp.bfloat16),
            pltpu.SemaphoreType.DMA((len(IN_PARTS),)),
            pltpu.SemaphoreType.DMA((len(OUT_PARTS),)),
        ],
        compiler_params=pltpu.CompilerParams(vmem_limit_bytes=16 * 1024 * 1024),
    )(index.reshape(-1, 128), table.reshape(Z * plane * held, part, block))
    panels = lax.all_to_all(picked.reshape(plane, count * part, block), PLANE, 0, 0, axis_index_groups=ORDER2, tiled=True)
    panels = panels.reshape(plane, count, part, block)
    half = block // 2
    core = lax.axis_index("aux").reshape(1)
    sent, kept, near_row = pl.pallas_call(
        turn_kernel,
        out_shape=[jax.ShapeDtypeStruct((count, half, inner), jnp.bfloat16)] * 2
        + [jax.ShapeDtypeStruct((1, count), jnp.int32)],
        in_specs=[pl.BlockSpec(memory_space=pltpu.SMEM)] + [pl.BlockSpec(memory_space=pltpu.VMEM)] * 2,
        out_specs=[pl.BlockSpec(memory_space=pltpu.VMEM)] * 3,
        cost_estimate=pl.CostEstimate(flops=0, bytes_accessed=4 * tiles.size, transcendentals=0),
        compiler_params=pltpu.CompilerParams(vmem_limit_bytes=8 * 1024 * 1024),
    )(core, tile_row.reshape(1, count), tiles)

    def row_sums(turned):
        return pl.pallas_call(
            sum_kernel,
            out_shape=jax.ShapeDtypeStruct((rows_local, half, block), jnp.float32),
            in_specs=[pl.BlockSpec(memory_space=pltpu.VMEM)] * 3,
            out_specs=pl.BlockSpec(memory_space=pltpu.VMEM),
            scratch_shapes=[
                pltpu.SMEM((1, count), jnp.int32),
                pltpu.VMEM((count, half, block), jnp.float32),
                pltpu.SemaphoreType.DMA,
            ],
            cost_estimate=pl.CostEstimate(
                flops=2 * tiles.size * half, bytes_accessed=4 * tiles.size, transcendentals=0
            ),
            compiler_params=pltpu.CompilerParams(vmem_limit_bytes=16 * 1024 * 1024),
        )(near_row, turned, panels)

    other = lax.ppermute(row_sums(sent), "aux", [(0, 1), (1, 0)])
    return row_sums(kept) + other


def solution(mesh):
    orbs, grps, cores = mesh.devices.shape
    split = Mesh(mesh.devices.reshape(orbs, grps // Z, Z, cores), ("orb", "x", "z", "aux"))
    own = ("orb", "x", "z")
    return jax.shard_map(
        shards,
        mesh=split,
        in_specs=(
            P(own, "aux", None),
            P(own, None),
            P(own),
            P(own),
            P("orb", ("x", "z"), "aux", None),
        ),
        out_specs=P(own, "aux", None),
        check_vma=False,
    )
```
